512 devices in a mesh: row: 32 (over x, y, core), col: 16 (over z).
Axes of the slice: x: 4, y: 4, z: 16, core: 2. Of those that a mesh axis runs over, the one named last changes fastest.
Arguments:
- hessian: float32 [2, 8192, 4, 4096], P(None, 'row', None, 'col'), as said below
- masses: float32 [16384], replicated, may hold values from 1 to 32
- shift: float32 [1], replicated, may hold values from 1 to 4
Outputs:
- factored: float32 [2, 8192, 4, 4096], P(None, 'row', None, 'col')
The draws below stay inside these ranges and needn't reach their ends.
Inputs may be any that keep to these rules, and one draw needn't show every extreme that they name: `hessian`: symmetric and positive definite.
All inputs are finite; a program needn't handle non-finite values.
Results may differ from the reference program's by a relative error of at most 0.0001.
Values sent between devices are 32-bit elements; how exact they have to be, the bound alone decides.
A program may use at most 64 MiB of HBM per device.

```python
import math
import jax
import jax.numpy as jnp
from jax import lax

N = 16384
NB = 256
PANELS = 2
KR = 2
KC = 4


def draw_hessian(key, part):
    key = jax.random.fold_in(key, 11)
    first, second = jax.random.split(key, 2)
    raw = jax.random.uniform(first, (N, N), jnp.float32, minval=-1.0, maxval=1.0)
    spread = 0.4083
    symmetric = 0.5 * (raw + raw.T)
    edge = 2.2 * spread * jnp.sqrt(jnp.float32(N))
    diagonal = edge * jax.random.uniform(second, (N,), jnp.float32, minval=1.0, maxval=1.3)
    diagonal_index = jnp.arange(N)
    symmetric = symmetric.at[diagonal_index, diagonal_index].set(diagonal)
    return symmetric.reshape(KR, N // KR, KC, N // KC)


def setup_inputs(seed: int = 0) -> dict:
    key_of = jax.random.split(jax.random.key(seed), 4)
    hessian = draw_hessian(jax.random.fold_in(key_of[3], 71), 0)
    masses = jnp.clip(jnp.exp(jax.random.uniform(key_of[1], (N,), jnp.float32, math.log(1.0), math.log(32.0))), 1.0, 32.0)
    shift = jnp.clip(jax.random.uniform(key_of[2], (1,), jnp.float32, 1.0, 4.0), 1.0, 4.0)
    return dict(hessian=hessian, masses=masses, shift=shift)


def reference(hessian, masses, shift):
    total = masses.shape[0]
    matrix = hessian.reshape(total, total)
    weight = 1.0 / jnp.sqrt(masses)
    matrix = matrix * weight[:, None] * weight[None, :]
    diagonal_index = jnp.arange(total)
    matrix = matrix.at[diagonal_index, diagonal_index].add(shift[0])
    for panel in range(PANELS):
        start = panel * NB
        stop = start + NB
        factor = jnp.linalg.cholesky(matrix[start:stop, start:stop])
        below = lax.linalg.triangular_solve(factor, matrix[stop:, start:stop], left_side=False, lower=True, transpose_a=True)
        trail = matrix[stop:, stop:] - jnp.dot(below, below.T, precision=lax.Precision.HIGHEST)
        matrix = matrix.at[stop:, stop:].set(trail)
        matrix = matrix.at[start:stop, start:stop].set(factor)
        matrix = matrix.at[stop:, start:stop].set(below)
        matrix = matrix.at[start:stop, stop:].set(jnp.zeros((NB, total - stop), matrix.dtype))
    return matrix.reshape(hessian.shape)
```

```python
import functools

import jax
import jax.numpy as jnp
from jax import lax
from jax.experimental import pallas as pl
from jax.experimental.pallas import tpu as pltpu
from jax.sharding import PartitionSpec as P

MESH = pl.DeviceIdType.MESH
HIGHEST = lax.Precision.HIGHEST
Z, R = 16, 32
NB = 256
CHUNKS = 8
ROWS = 512 // CHUNKS
PIVOTS = ((0, 0), (0, 1), (1, 1))


def eight(i):
    return pl.ds(pl.multiple_of(8 * i, 8), 8)


def wait_for(ref, sem):
    pltpu.make_async_copy(ref, ref, sem).wait()


def lane(x, i):
    return jnp.broadcast_to(x[:, i : i + 1], (8, 128))


def sublane(x, i):
    return jnp.broadcast_to(x[i : i + 1, :], (8, x.shape[1]))


def tree_sum(terms):
    while len(terms) > 1:
        terms = [terms[i] + terms[i + 1] for i in range(0, len(terms), 2)]
    return terms[0]


def factor8(tile, off):
    s, low, inv = {}, {}, {}
    for k in range(8):
        column = lane(tile, off + k)
        for i in range(k, 8):
            s[i, k] = sublane(column, i)
    for j in range(8):
        root = lax.rsqrt(s[j, j])
        for i in range(j + 1, 8):
            low[i, j] = s[i, j] * root
        for k in range(j + 1, 8):
            for i in range(k, 8):
                s[i, k] = s[i, k] - low[i, j] * low[k, j]
        inv[j, j] = root
        for c in range(j):
            total = low[j, c] * inv[c, c]
            for k in range(c + 1, j):
                total = total + low[j, k] * inv[k, c]
            inv[j, c] = -(total * root)
    row = lax.broadcasted_iota(jnp.int32, (8, 128), 0)
    columns = []
    for c in range(8):
        x = jnp.zeros((8, 128), jnp.float32)
        for i in range(c, 8):
            x = jnp.where(row == i, inv[i, c], x)
        columns.append(x)
    return columns


def combine(columns, x):
    return tree_sum([columns[j] * sublane(x, j) for j in range(8)])


def factor128(block, upper_ref, inverse_ref, pump):
    rows = lax.broadcasted_iota(jnp.int32, (8, 128), 0)
    lanes = lax.broadcasted_iota(jnp.int32, (8, 128), 1)
    d = [block[8 * t : 8 * t + 8, :] for t in range(16)]
    e = [jnp.where(lanes == rows + 8 * t, 1.0, 0.0) for t in range(16)]
    for t in range(16):
        columns = factor8(d[t], 8 * t)
        u = combine(columns, d[t])
        f = combine(columns, e[t])
        upper_ref[8 * t : 8 * t + 8, :] = jnp.where(lanes >= rows + 8 * t, u, 0.0)
        inverse_ref[8 * t : 8 * t + 8, :] = f
        if t % 4 == 3:
            pump(t // 4)
        if t == 15:
            break
        v = u.T
        ub = [sublane(u, j) for j in range(8)]
        fb = [sublane(f, j) for j in range(8)]
        for q in range(t + 1, 16):
            vq = v[8 * q : 8 * q + 8, :]
            g = [lane(vq, j) for j in range(8)]
            d[q] = d[q] - tree_sum([g[j] * ub[j] for j in range(8)])
            e[q] = e[q] - tree_sum([g[j] * fb[j] for j in range(8)])


def split(x):
    high = x.astype(jnp.bfloat16)
    return high, (x - high.astype(jnp.float32)).astype(jnp.bfloat16)


def dot(a, b):
    return jnp.dot(a, b, preferred_element_type=jnp.float32)


def kernel(x, out, piv, rb, cb, w, ud, md, below, across,
           s_a, r_a, s_b, r_b, s_c, r_c, s_1, r_1, s_2, r_2, s_z, r_z):
    r, z = lax.axis_index("row"), lax.axis_index("col")

    def at_row(i):
        return (lax.rem(r + i, R), z)

    def at_col(i):
        return (r, lax.rem(z + i + Z, Z))

    barrier = pltpu.get_barrier_semaphore()

    def greet_col(i, carry):
        pl.semaphore_signal(barrier, inc=1, device_id=at_col(i), device_id_type=MESH)
        return carry

    def greet_row(i, carry):
        pl.semaphore_signal(barrier, inc=1, device_id=at_row(i), device_id_type=MESH)
        return carry

    lax.fori_loop(1, Z, greet_col, 0)
    lax.fori_loop(1, R, greet_row, 0)
    pl.semaphore_wait(barrier, Z - 1 + R - 1)

    def send(src, dst, send_sem, recv_sem, device):
        pltpu.make_async_remote_copy(src, dst, send_sem, recv_sem, device_id=device, device_id_type=MESH).start()

    def each(count, fn):
        def body(i, carry):
            fn(i)
            return carry
        lax.fori_loop(1, count, body, 0)

    for b, (rs, zs) in enumerate(PIVOTS):
        @pl.when((r == rs) & (z == zs))
        def _():
            each(R, lambda i: send(x.at[0, 0, eight(lax.rem(rs + i, R))], piv.at[b, eight(lax.rem(rs + i, R))],
                                   s_a.at[b], r_a.at[b], at_row(i)))
            piv[b, 8 * rs : 8 * rs + 8, :] = x[0, 0, 8 * rs : 8 * rs + 8, :]

    for b in range(2):
        @pl.when(r == b)
        def _():
            each(R, lambda i: send(x.at[0, :, eight(lax.rem(b + i, R))], rb.at[b, :, eight(lax.rem(b + i, R))],
                                   s_1.at[b], r_1.at[b], at_row(i)))
            rb[b, :, 8 * b : 8 * b + 8, :] = x[0, :, 8 * b : 8 * b + 8, :]

    for b, (rs, zs) in enumerate(PIVOTS):
        mine = piv.at[b, eight(r)]

        @pl.when((z == zs) & (r != rs))
        def _():
            wait_for(mine, r_a.at[b])

        @pl.when(z == zs)
        def _():
            each(Z, lambda i: send(mine, mine, s_b.at[b], r_b.at[b], at_col(i)))

        @pl.when(z != zs)
        def _():
            wait_for(mine, r_b.at[b])

        each(R, lambda i: send(mine, mine, s_c.at[b], r_c.at[b], at_row(i)))

    for p in range(2):
        @pl.when(z == p)
        def _():
            cb[p, 0:NB, :] = x[0, 0]
            cb[p, NB : 2 * NB, :] = x[1, 0]

    def pump(chunk, p):
        zp = lax.rem(z + Z - p, Z)
        piece = cb.at[p, pl.ds(pl.multiple_of(chunk * ROWS, ROWS), ROWS)]

        @pl.when(zp != 0)
        def _():
            wait_for(piece, r_z.at[p, chunk])

        @pl.when(lax.rem(zp, 2) == 0)
        def _():
            forward = jnp.where(zp < 8, 2, jnp.where(zp == 10, -1, -2))
            back = jnp.where(zp == 0, -2, jnp.where(zp <= 8, -1, 1))

            @pl.when(zp != 8)
            def _():
                send(piece, piece, s_z.at[p], r_z.at[p, chunk], at_col(forward))

            send(piece, piece, s_z.at[p], r_z.at[p, chunk], at_col(back))

    for b in range(2):
        mine = rb.at[b, :, eight(r)]

        @pl.when(r != b)
        def _():
            wait_for(mine, r_1.at[b])

        each(R, lambda i: send(mine, mine, s_2.at[b], r_2.at[b], at_row(i)))

    all_but = pl.ds(0, 248)
    for b in range(3):
        wait_for(piv.at[b, all_but], r_c.at[b])

    w[...] = jnp.zeros_like(w)
    w[0:NB, 0:NB] = piv[0]
    w[0:NB, NB : 2 * NB] = piv[1]
    w[NB : 2 * NB, NB : 2 * NB] = piv[2]

    def step(k, carry):
        mine = pl.ds(pl.multiple_of(k * 128, 128), 128)
        window = pl.ds(pl.multiple_of(k * 128, 128), 640)
        factor128(w.at[mine, mine], ud.at[k], md, lambda i: pump(lax.rem(4 * k + i, 8), lax.div(k, 2)))
        w[mine, pl.ds(pl.multiple_of(512 + k * 128, 128), 128)] = jnp.where(
            lax.broadcasted_iota(jnp.int32, (128, 128), 0) == lax.broadcasted_iota(jnp.int32, (128, 128), 1), 1.0, 0.0)
        row = jnp.dot(md[...], w[mine, window], precision=HIGHEST)
        w[mine, window] = row

        def update(i, c):
            there = pl.ds(pl.multiple_of(i * 128, 128), 128)
            w[there, window] = w[there, window] - jnp.dot(w[mine, there].T, w[mine, window], precision=HIGHEST)
            return c

        lax.fori_loop(k + 1, 4, update, 0)
        return carry

    lax.fori_loop(0, 4, step, 0)

    for b in range(2):
        wait_for(rb.at[b, :, all_but], r_2.at[b])
    m0, m1 = w[0:NB, 512:768], w[NB : 2 * NB, 512:1024]
    nt = (((1,), (1,)), ((), ()))

    def solve_below(k, carry):
        here = pl.ds(pl.multiple_of(k * NB, NB), NB)
        c0, c1 = cb[0, here], cb[1, here]
        below[here, 0:NB] = lax.dot_general(c0, m0, nt, precision=HIGHEST)
        below[here, NB : 2 * NB] = (lax.dot_general(c0, m1[:, 0:NB], nt, precision=HIGHEST)
                                    + lax.dot_general(c1, m1[:, NB : 2 * NB], nt, precision=HIGHEST))
        return carry

    lax.fori_loop(0, 2, solve_below, 0)

    def solve_across(c, carry):
        r0, r1 = rb[0, c], rb[1, c]
        across[c, 0:NB] = jnp.dot(m0, r0, precision=HIGHEST)
        across[c, NB : 2 * NB] = (jnp.dot(m1[:, 0:NB], r0, precision=HIGHEST)
                                  + jnp.dot(m1[:, NB : 2 * NB], r1, precision=HIGHEST))
        return carry

    lax.fori_loop(0, 4, solve_across, 0)

    def product(i, carry):
        k, c = lax.div(i, 4), lax.rem(i, 4)
        here = pl.ds(pl.multiple_of(k * NB, NB), NB)
        bh, bl = split(below[here])
        ah, al = split(across[c])
        out[k, c] = x[k, c] - (dot(bh, ah) + dot(bh, al) + dot(bl, ah))
        return carry

    lax.fori_loop(0, 8, product, 0)

    for p in range(2):
        @pl.when(z == p)
        def _():
            for k in range(2):
                out[k, 0] = below[NB * k : NB * k + NB, NB * p : NB * p + NB]

    for p in range(2):
        @pl.when(r == p)
        def _():
            for c in range(1, 4):
                out[0, c] = jnp.zeros((NB, NB), jnp.float32)

            @pl.when(z > p)
            def _():
                out[0, 0] = jnp.zeros((NB, NB), jnp.float32)

            @pl.when(z == p)
            def _():
                out[0, 0, 0:128, 0:128] = ud[2 * p].T
                out[0, 0, 0:128, 128:256] = jnp.zeros((128, 128), jnp.float32)
                out[0, 0, 128:256, 0:128] = w[256 * p : 256 * p + 128, 256 * p + 128 : 256 * p + 256].T
                out[0, 0, 128:256, 128:256] = ud[2 * p + 1].T

    for b, (rs, zs) in enumerate(PIVOTS):
        @pl.when((r == rs) & (z == zs))
        def _():
            wait_for(piv.at[b, all_but], s_a.at[b])

        @pl.when(z == zs)
        def _():
            wait_for(piv.at[b, pl.ds(0, 120)], s_b.at[b])

        wait_for(piv.at[b, all_but], s_c.at[b])
    for b in range(2):
        @pl.when(r == b)
        def _():
            wait_for(rb.at[b, :, all_but], s_1.at[b])

        wait_for(rb.at[b, :, all_but], s_2.at[b])
    for p in range(2):
        zp = lax.rem(z + Z - p, Z)

        @pl.when(lax.rem(zp, 2) == 0)
        def _():
            wait_for(cb.at[p], s_z.at[p])

            @pl.when(zp != 8)
            def _():
                wait_for(cb.at[p], s_z.at[p])


def shards(hessian, masses, shift):
    row_index, col_index = lax.axis_index("row"), lax.axis_index("col")
    weight = 1.0 / jnp.sqrt(masses)
    row_weight = lax.dynamic_index_in_dim(weight.reshape(2, R, NB), row_index, 1, keepdims=False)
    col_weight = lax.dynamic_index_in_dim(weight.reshape(4, Z, NB), col_index, 1, keepdims=False)
    row_cells = (jnp.arange(2) * R + row_index)[:, None] * NB + jnp.arange(NB)[None, :]
    col_cells = (jnp.arange(4) * Z + col_index)[:, None] * NB + jnp.arange(NB)[None, :]
    on_diagonal = row_cells[:, None, :, None] == col_cells[None, :, None, :]
    matrix = hessian.transpose(0, 2, 1, 3) * row_weight[:, None, :, None] * col_weight[None, :, None, :]
    matrix = matrix + jnp.where(on_diagonal, shift[0], 0.0)
    dma = pltpu.SemaphoreType.DMA
    f32 = jnp.float32
    factored = pl.pallas_call(
        kernel,
        out_shape=jax.ShapeDtypeStruct((2, 4, NB, NB), f32),
        in_specs=[pl.BlockSpec(memory_space=pltpu.VMEM)],
        out_specs=pl.BlockSpec(memory_space=pltpu.VMEM),
        scratch_shapes=[
            pltpu.VMEM((3, NB, NB), f32),
            pltpu.VMEM((2, 4, NB, NB), f32),
            pltpu.VMEM((2, 512, NB), f32),
            pltpu.VMEM((512, 1024), f32),
            pltpu.VMEM((4, 128, 128), f32),
            pltpu.VMEM((128, 128), f32),
            pltpu.VMEM((512, 512), f32),
            pltpu.VMEM((4, 512, NB), f32),
            dma((3,)), dma((3,)), dma((3,)), dma((3,)), dma((3,)), dma((3,)),
            dma((2,)), dma((2,)), dma((2,)), dma((2,)),
            dma((2,)), dma((2, CHUNKS)),
        ],
        compiler_params=pltpu.CompilerParams(collective_id=0, has_side_effects=True, vmem_limit_bytes=48 * 2**20),
    )(matrix)
    return factored.transpose(0, 2, 1, 3)


def solution(mesh):
    placed = (P(None, "row", None, "col"), P(), P())
    return jax.shard_map(
        shards, mesh=mesh, in_specs=placed, out_specs=P(None, "row", None, "col"), check_vma=False
    )
```

```python
import functools

import jax
import jax.numpy as jnp
from jax import lax
from jax.experimental import pallas as pl
from jax.experimental.pallas import tpu as pltpu
from jax.sharding import PartitionSpec as P

MESH = pl.DeviceIdType.MESH
HIGHEST = lax.Precision.HIGHEST
Z, R = 16, 32
NB = 256
CHUNKS = 16
ROWS = 1024 // CHUNKS


def wait_for(ref, sem):
    pltpu.make_async_copy(ref, ref, sem).wait()


def lane(x, i):
    return jnp.broadcast_to(x[:, i : i + 1], (8, 128))


def sublane(x, i):
    return jnp.broadcast_to(x[i : i + 1, :], (8, x.shape[1]))


def tree_sum(terms):
    while len(terms) > 1:
        terms = [terms[i] + terms[i + 1] for i in range(0, len(terms), 2)]
    return terms[0]


def factor8(tile, off):
    s, low, inv = {}, {}, {}
    for k in range(8):
        column = lane(tile, off + k)
        for i in range(k, 8):
            s[i, k] = sublane(column, i)
    for j in range(8):
        root = lax.rsqrt(s[j, j])
        for i in range(j + 1, 8):
            low[i, j] = s[i, j] * root
        for k in range(j + 1, 8):
            for i in range(k, 8):
                s[i, k] = s[i, k] - low[i, j] * low[k, j]
        inv[j, j] = root
        for c in range(j):
            total = low[j, c] * inv[c, c]
            for k in range(c + 1, j):
                total = total + low[j, k] * inv[k, c]
            inv[j, c] = -(total * root)
    row = lax.broadcasted_iota(jnp.int32, (8, 128), 0)
    columns = []
    for c in range(8):
        x = jnp.zeros((8, 128), jnp.float32)
        for i in range(c, 8):
            x = jnp.where(row == i, inv[i, c], x)
        columns.append(x)
    return columns


def combine(columns, x):
    return tree_sum([columns[j] * sublane(x, j) for j in range(8)])


def factor128(block, inverse_ref, done):
    rows = lax.broadcasted_iota(jnp.int32, (8, 128), 0)
    lanes = lax.broadcasted_iota(jnp.int32, (8, 128), 1)
    d = [block[8 * t : 8 * t + 8, :] for t in range(16)]
    e = [jnp.where(lanes == rows + 8 * t, 1.0, 0.0) for t in range(16)]
    for t in range(16):
        columns = factor8(d[t], 8 * t)
        u = combine(columns, d[t])
        f = combine(columns, e[t])
        inverse_ref[8 * t : 8 * t + 8, :] = f
        done(t)
        if t == 15:
            break
        v = u.T
        ub = [sublane(u, j) for j in range(8)]
        fb = [sublane(f, j) for j in range(8)]
        for q in range(t + 1, 16):
            vq = v[8 * q : 8 * q + 8, :]
            g = [lane(vq, j) for j in range(8)]
            d[q] = d[q] - tree_sum([g[j] * ub[j] for j in range(8)])
            e[q] = e[q] - tree_sum([g[j] * fb[j] for j in range(8)])


def split(x):
    high = x.astype(jnp.bfloat16)
    return high, (x - high.astype(jnp.float32)).astype(jnp.bfloat16)


def dot(a, b):
    return jnp.dot(a, b, preferred_element_type=jnp.float32)


NAMES = {}
_TOTAL = 0
for _name, _count in (("x", 2), ("fc", 2), ("fb", 4), ("pc", 4), ("r1s", 2), ("r1r", 2), ("r2s", 2), ("r2r", 2), ("rfs", 2), ("rfr", 2),
                      ("as", 4), ("ar", 4), ("bs", 4), ("br", 4), ("cs", 4), ("cr", 4), ("ss", 4), ("sr", 4),
                      ("zs", 2), ("ps", 1), ("zr", 2 * CHUNKS)):
    NAMES[_name] = _TOTAL
    _TOTAL += _count
SEMAPHORES = _TOTAL


def rows16(i):
    return pl.ds(pl.multiple_of(16 * i, 16), 16)


def kernel(shift, h, masses, out, x, acc, rb, cb, fb, tb, w, g, wc, wr, bel, acr, mi, u, ut, sems, ready_z, ready_p, ready_b):
    r, z = lax.axis_index("row"), lax.axis_index("col")
    chip, core = lax.div(r, 2), lax.rem(r, 2)
    even = core == 0
    first = (r == 0) & (z == 0)
    second = (r == 1) & (z == 0)
    odd = core == 1
    sibling = (r + 1 - 2 * core, z)
    zp = [z, lax.rem(z + Z - 1, Z)]

    def sem(name, i=0):
        return sems.at[NAMES[name] + i]

    def col(offset, row=None):
        return (r if row is None else row, lax.rem(z + offset + Z, Z))

    def chip_at(i):
        return (2 * i + core, z)

    def send(src, dst, send_sem, recv_sem, device):
        pltpu.make_async_remote_copy(src, dst, send_sem, recv_sem, device_id=device, device_id_type=MESH).start()

    def signal(s, device):
        pl.semaphore_signal(s, inc=1, device_id=device, device_id_type=MESH)

    def each(low, high, fn):
        def body(i, carry):
            fn(i)
            return carry
        lax.fori_loop(low, high, body, 0)

    def pick(value, cases, default=0):
        result = default
        for key, v in cases.items():
            result = jnp.where(value == key, v, result)
        return result

    def children(p):
        v = zp[p]
        skip = {} if p == 1 else {15: -2}
        fwd = pick(v, {0: 1, 1: 2, 3: 2, 5: 2, 7: 1, 13: -2, 11: -2, 9: 1, **skip})
        back = pick(v, {0: -1, 3: -1, 5: -1, 7: -1, 13: 1, 11: 1})
        far = pick(v, {0: -3}) if p == 1 else None
        return fwd, back, far

    def parent(p):
        v = zp[p]
        offset = pick(v, {1: -1, 15: 1, 3: -2, 5: -2, 7: -2, 8: -1, 2: 1, 4: 1, 6: 1, 13: 2 if p == 0 else 3, 11: 2, 9: 2,
                          14: -1, 12: -1, 10: -1})
        slot = pick(v, {15: 1, 2: 1, 4: 1, 6: 1, 14: 1, 12: 1, 13: 0 if p == 0 else 2})
        return offset, slot

    kids = [children(0), children(1)]
    from_proxy = (r == 0) & ((z == 1) | (z == 15))

    barrier = pltpu.get_barrier_semaphore()
    signal(barrier, sibling)

    @pl.when(odd)
    def _():
        each(1, 16, lambda i: signal(barrier, chip_at(lax.rem(chip + i, 16))))

    @pl.when(odd & (chip != 0) & (z == 0))
    def _():
        signal(barrier, (0, 0))

    for p in range(2):
        own = even & jnp.logical_not(first) if p == 0 else even
        for offset in kids[p]:
            if offset is not None:
                @pl.when((offset != 0) & own)
                def _():
                    signal(barrier, col(offset))

    @pl.when(second)
    def _():
        signal(barrier, (0, 1))
        signal(barrier, (0, 15))

    @pl.when(odd & (z == 0))
    def _():
        each(1, Z, lambda i: signal(barrier, col(i)))

    one = jnp.int32(1)
    zero = jnp.int32(0)
    expected = (one + jnp.where(first, 15, 0) + jnp.where(odd, 15, 0)
                + jnp.where(even & (zp[0] != 0), one, zero) + jnp.where(even & (zp[1] != 0), one, zero) + jnp.where(odd & (z != 0), one, zero))

    def weights(block):
        return 1.0 / jnp.sqrt(masses[pl.ds(2 * block, 2), :])

    across_weights = [weights(z + Z * c) for c in range(4)]
    square = lax.broadcasted_iota(jnp.int32, (NB, NB), 0) == lax.broadcasted_iota(jnp.int32, (NB, NB), 1)
    for k in range(2):
        down = weights(r + R * k)
        for half in range(2):
            tall = jnp.broadcast_to(down[half : half + 1, :], (128, 128)).T
            rows = slice(128 * half, 128 * half + 128)
            for c in range(4):
                for side in range(2):
                    cols = slice(128 * side, 128 * side + 128)
                    x[k, c, rows, cols] = h[k, rows, c, cols] * tall * across_weights[c][side : side + 1, :]
        for c in range(4):
            @pl.when(r + R * k == z + Z * c)
            def _():
                x[k, c] = x[k, c] + jnp.where(square, shift[0], 0.0)

    pl.semaphore_wait(barrier, expected)

    for p in range(2):
        offset, slot = parent(p)
        for s in range(3 if p == 1 else 2):
            if p == 0:
                @pl.when(even & (zp[p] != 0) & (slot == s) & jnp.logical_not(from_proxy))
                def _():
                    signal(ready_z.at[p, s], col(offset))
            else:
                @pl.when(even & (zp[p] != 0) & (slot == s))
                def _():
                    signal(ready_z.at[p, s], col(offset))

    @pl.when((r == 0) & (z == 1))
    def _():
        signal(ready_p.at[0], (1, 0))

    @pl.when((r == 0) & (z == 15))
    def _():
        signal(ready_p.at[1], (1, 0))

    @pl.when(odd & (z != 0))
    def _():
        signal(ready_b, (r, 0))

    def chunk_of(i):
        return pl.ds(pl.multiple_of(i * ROWS, ROWS), ROWS)

    def chain_send(p, i, offset):
        piece = cb.at[p, chunk_of(i)]
        send(piece, piece, sem("zs", p), sem("zr", p * CHUNKS + i), col(offset))

    def all_chunks(p, slot, offset):
        pl.semaphore_wait(ready_z.at[p, slot], 1)
        each(0, CHUNKS, lambda i: chain_send(p, i, offset))

    def pumps(p, between=None):
        fwd, back, _ = kids[p]

        @pl.when(fwd != 0)
        def _():
            pl.semaphore_wait(ready_z.at[p, 0], 1)

        @pl.when(back != 0)
        def _():
            pl.semaphore_wait(ready_z.at[p, 1], 1)

        def pump(i):
            wait_for(cb.at[p, chunk_of(i)], sem("zr", p * CHUNKS + i))

            @pl.when(fwd != 0)
            def _():
                chain_send(p, i, fwd)

            @pl.when(back != 0)
            def _():
                chain_send(p, i, back)

        if between is None:
            each(0, CHUNKS, pump)
        else:
            each(0, CHUNKS // 2, pump)
            between()
            each(CHUNKS // 2, CHUNKS, pump)
        theirs = cb.at[p, pl.ds(512, 512)]
        send(theirs, cb.at[p, pl.ds(0, 512)], sem("pc", 2 * p), sem("pc", 2 * p + 1), sibling)

    def width(k):
        return pl.ds(0, 512 - 128 * k)

    def slab(k, i):
        return g.at[k, pl.ds(pl.multiple_of(8 * i, 8), 8), width(k)]

    def g_relay(k):
        piece = slab(k, chip)

        @pl.when(second)
        def _():
            wait_for(g.at[k, :, width(k)], sem("sr", k))

        @pl.when((z == 0) & (chip != 0))
        def _():
            wait_for(piece, sem("ar", k))

        @pl.when(z == 0)
        def _():
            if k == 0:
                pl.semaphore_wait(ready_b, Z - 1)
            each(1, Z, lambda i: send(piece, piece, sem("bs", k), sem("br", k), (r, 1 + lax.rem(i + 6, Z - 1))))

        @pl.when(z != 0)
        def _():
            wait_for(piece, sem("br", k))

        def spread(i):
            there = lax.rem(chip + i, 16)

            @pl.when((z != 0) | (there != 0))
            def _():
                send(piece, piece, sem("cs", k), sem("cr", k), chip_at(there))

        each(1, 16, spread)

    def g_arrive(k):
        whole = g.at[k, :, width(k)]

        @pl.when(jnp.logical_not(second))
        def _():
            wait_for(g.at[k, pl.ds(0, 120), width(k)], sem("cr", k))
            send(whole, whole, sem("ss", k), sem("sr", k), sibling)

    nt = (((1,), (1,)), ((), ()))

    def load_rows():
        for b in range(2):
            for c in range(4):
                wr[NB * b : NB * b + NB, NB * c : NB * c + NB] = rb[b, c]

    def invert(q):
        top, bottom = g[2 * q, :, 0:128], g[2 * q + 1, :, 0:128]
        mi[0:128, 0:128] = top
        mi[0:128, 128:256] = jnp.zeros((128, 128), jnp.float32)
        mi[128:256, 128:256] = bottom
        inner = jnp.dot(g[2 * q, :, 128:256].T, top, precision=HIGHEST)
        mi[128:256, 0:128] = -jnp.dot(bottom, inner, precision=HIGHEST)

    def solve_across(q):
        def body(c, carry):
            cols = pl.ds(pl.multiple_of(c * NB, NB), NB)
            acr[NB * q : NB * q + NB, cols] = jnp.dot(mi[...], wr[NB * q : NB * q + NB, cols], precision=HIGHEST)
            return carry
        lax.fori_loop(0, 4, body, 0)

    def solve_below(q):
        def body(k, carry):
            rows = pl.ds(pl.multiple_of(k * NB, NB), NB)
            here = slice(NB * q, NB * q + NB)
            bel[rows, here] = lax.dot_general(wc[rows, here], mi[...], nt, precision=HIGHEST)
            return carry
        lax.fori_loop(0, 2, body, 0)

    def update():
        u[0:128, :] = g[0, :, 256:512]
        u[128:256, :] = g[1, :, 128:384]
        ut[...] = u[...].T

        def below_part(k, carry):
            rows = pl.ds(pl.multiple_of(k * NB, NB), NB)
            wc[rows, NB : 2 * NB] = -jnp.dot(bel[rows, 0:NB], u[...], precision=HIGHEST)
            return carry
        lax.fori_loop(0, 2, below_part, 0)

        def across_part(c, carry):
            cols = pl.ds(pl.multiple_of(c * NB, NB), NB)
            wr[NB : 2 * NB, cols] = wr[NB : 2 * NB, cols] - jnp.dot(ut[...], acr[0:NB, cols], precision=HIGHEST)
            return carry
        lax.fori_loop(0, 4, across_part, 0)

    def product(q):
        def body(k, carry):
            rows = pl.ds(pl.multiple_of(k * NB, NB), NB)
            bh, bl = split(bel[rows, NB * q : NB * q + NB])
            for c in range(4):
                ah, al = split(acr[NB * q : NB * q + NB, NB * c : NB * c + NB])
                term = dot(bh, ah) + dot(bh, al) + dot(bl, ah)
                if q == 0:
                    acc[k, c] = x[k, c] - term
                else:
                    out[k, :, c, :] = acc[k, c] - term
            return carry
        lax.fori_loop(0, 2, body, 0)

    @pl.when(first)
    def _():
        send(x.at[0], rb.at[0], sem("x", 0), sem("x", 1), sibling)
        for k in range(2):
            send(x.at[k, 0], cb.at[0, pl.ds(NB * k, NB)], sem("fc", 0), sem("fc", 1), sibling)
        w[0:NB, 0:NB] = x[0, 0]

        def step(k, carry):
            mine = pl.ds(pl.multiple_of(k * 128, 128), 128)
            window = pl.ds(pl.multiple_of(k * 128 + 128, 128), 384)

            @pl.when(k == 2)
            def _():
                u[0:128, :] = g[0, :, 256:512]
                u[128:256, :] = g[1, :, 128:384]
                wait_for(fb.at[1], sem("fb", 3))
                w[NB : 2 * NB, NB : 2 * NB] = fb[1] - jnp.dot(u[...].T, u[...], precision=HIGHEST)

            def last(t):
                if t > 0:
                    @pl.when(k == 3)
                    def _():
                        send(slab(3, t), slab(3, t), sem("as", 3), sem("ar", 3), (2 * t + 1, z))

            factor128(w.at[mine, mine], g.at[k, :, pl.ds(0, 128)], last)

            @pl.when(k == 0)
            def _():
                wait_for(fb.at[0], sem("fb", 2))
                w[0:NB, NB : 2 * NB] = fb[0]

            @pl.when(k < 3)
            def _():
                g[k, :, 128:512] = jnp.dot(g[k, :, 0:128], w[mine, window], precision=HIGHEST)

            for n in range(4):
                @pl.when(k == n)
                def _():
                    if n < 3:
                        each(1, 16, lambda i: send(slab(n, i), slab(n, i), sem("as", n), sem("ar", n), (2 * i + 1, z)))
                    whole = g.at[n, :, width(n)]
                    send(whole, whole, sem("ss", n), sem("sr", n), sibling)

            @pl.when(lax.rem(k, 2) == 0)
            def _():
                there = pl.ds(pl.multiple_of(k * 128 + 128, 128), 128)
                w[there, window] = w[there, window] - jnp.dot(g[k, :, 128:256].T, g[k, :, 128:512], precision=HIGHEST)

            return carry

        lax.fori_loop(0, 4, step, 0)

    @pl.when((r == 0) & (z != 0))
    def _():
        send(x.at[0], rb.at[0], sem("x", 0), sem("x", 1), sibling)

    @pl.when(second)
    def _():
        tb[...] = x[0, 0].T
        send(tb, fb.at[0], sem("fb", 0), sem("fb", 2), sibling)

    for p in range(2):
        @pl.when((z == p) & (core == 1) & jnp.logical_not(second))
        def _():
            for k in range(2):
                send(x.at[k, 0], cb.at[p, pl.ds(512 + NB * k, NB)], sem("fc", 0), sem("fc", 1), sibling)

    @pl.when(r == 0)
    def _():
        rb[0] = x[0]

    @pl.when(r == 1)
    def _():
        rb[1] = x[0]

    def scatter(b):
        def body(i):
            piece = rb.at[b, :, rows16(i)]
            send(piece, piece, sem("r1s", b), sem("r1r", b), chip_at(i))
        each(1, 16, body)

    def gather(b):
        mine = rb.at[b, :, rows16(chip)]

        @pl.when(chip != 0)
        def _():
            wait_for(mine, sem("r1r", b))

        def spread(i):
            there = lax.rem(chip + i, 16)

            @pl.when(there != 0)
            def _():
                send(mine, mine, sem("r2s", b), sem("r2r", b), chip_at(there))

        each(1, 16, spread)

    @pl.when(r == 1)
    def _():
        scatter(1)
        wait_for(rb.at[0], sem("x", 1))
        scatter(0)

    def proxy(slot, device):
        pl.semaphore_wait(ready_p.at[slot], 1)

        def body(i):
            piece = cb.at[0, chunk_of(i)]
            send(piece, piece, sem("ps"), sem("zr", i), device)
        each(0, CHUNKS, body)

    @pl.when(second)
    def _():
        for k in range(2):
            cb[0, 512 + NB * k : 512 + NB * k + NB, :] = x[k, 0]
        wait_for(cb.at[0, pl.ds(0, 512)], sem("fc", 1))
        proxy(0, (0, 1))

    @pl.when(core == 1)
    def _():
        gather(1)
        gather(0)

    @pl.when(second)
    def _():
        proxy(1, (0, 15))

    for p in range(2):
        @pl.when((z == p) & even & jnp.logical_not(first))
        def _():
            for k in range(2):
                cb[p, NB * k : NB * k + NB, :] = x[k, 0]
            wait_for(cb.at[p, pl.ds(512, 512)], sem("fc", 1))

    @pl.when((z == 0) & even & jnp.logical_not(first))
    def _():
        all_chunks(0, 0, 1)
        all_chunks(0, 1, -1)

    @pl.when((z == 1) & even)
    def _():
        pl.semaphore_wait(ready_z.at[1, 1], 1)

        @pl.when(r == 0)
        def _():
            send(cb.at[1, pl.ds(512, NB)], fb.at[1], sem("fb", 1), sem("fb", 3), (0, 0))

        each(0, CHUNKS, lambda i: chain_send(1, i, -1))
        all_chunks(1, 0, 1)

    @pl.when((z == 1) & even)
    def _():
        pumps(0, lambda: all_chunks(1, 2, -3))

    @pl.when((z > 1) & even)
    def _():
        pumps(0)

    leaf = (kids[1][0] == 0) & (kids[1][1] == 0)

    @pl.when((z != 1) & even & jnp.logical_not(leaf))
    def _():
        pumps(1)

    def rows_arrive(b):
        @pl.when(core == 1)
        def _():
            @pl.when(chip != 0)
            def _():
                wait_for(rb.at[b, :, pl.ds(0, 240)], sem("r2r", b))

            if b == 0:
                @pl.when(chip != 0)
                def _():
                    send(rb.at[b], rb.at[b], sem("rfs", b), sem("rfr", b), sibling)
            else:
                send(rb.at[b], rb.at[b], sem("rfs", b), sem("rfr", b), sibling)

    late = z >= 3

    @pl.when(odd)
    def _():
        g_relay(0)
        g_relay(1)
        rows_arrive(1)
        rows_arrive(0)
        g_arrive(0)
        g_relay(2)
        g_arrive(1)

        @pl.when(late)
        def _():
            g_relay(3)
            g_arrive(2)
            g_arrive(3)

    @pl.when(even)
    def _():
        wait_for(rb.at[1], sem("rfr", 1))

        @pl.when(chip != 0)
        def _():
            wait_for(rb.at[0], sem("rfr", 0))

    load_rows()

    def load_column(p):
        @pl.when(odd & (z != p))
        def _():
            wait_for(cb.at[p, pl.ds(0, 512)], sem("pc", 2 * p + 1))

        here = slice(NB * p, NB * p + NB)
        for k in range(2):
            rows = slice(NB * k, NB * k + NB)
            old = wc[rows, here] if p else 0.0

            @pl.when(z == p)
            def _():
                wc[rows, here] = x[k, 0] + old

            @pl.when(z != p)
            def _():
                wc[rows, here] = cb[p, rows, :] + old

    load_column(0)

    def slabs_arrive(q):
        @pl.when(even & jnp.logical_not(first))
        def _():
            for k in (2 * q, 2 * q + 1):
                wait_for(g.at[k, :, width(k)], sem("sr", k))

    slabs_arrive(0)
    invert(0)
    solve_across(0)
    solve_below(0)
    update()
    product(0)

    @pl.when(odd & jnp.logical_not(late))
    def _():
        g_relay(3)
        g_arrive(2)
        g_arrive(3)

    @pl.when((z != 1) & even & leaf)
    def _():
        pumps(1)

    load_column(1)
    slabs_arrive(1)
    invert(1)
    solve_across(1)
    solve_below(1)
    product(1)

    tri = lax.broadcasted_iota(jnp.int32, (NB, NB), 0) >= lax.broadcasted_iota(jnp.int32, (NB, NB), 1)
    for p in range(2):
        @pl.when(z == p)
        def _():
            for k in range(2):
                out[k, :, 0, :] = bel[NB * k : NB * k + NB, NB * p : NB * p + NB]

    for p in range(2):
        @pl.when(r == p)
        def _():
            for c in range(1, 4):
                out[0, :, c, :] = jnp.zeros((NB, NB), jnp.float32)

            @pl.when(z > p)
            def _():
                out[0, :, 0, :] = jnp.zeros((NB, NB), jnp.float32)

            @pl.when(z == p)
            def _():
                out[0, :, 0, :] = jnp.where(tri, bel[0:NB, NB * p : NB * p + NB], 0.0)

    @pl.when(r == 0)
    def _():
        wait_for(x.at[0], sem("x", 0))

    @pl.when(first)
    def _():
        wait_for(cb.at[0, pl.ds(0, 512)], sem("fc", 0))
        for k in range(4):
            wait_for(g.at[k, pl.ds(0, 120), width(k)], sem("as", k))

    @pl.when(second)
    def _():
        wait_for(tb, sem("fb", 0))
        wait_for(rb, sem("ps"))

    for p in range(2):
        @pl.when((z == p) & (core == 1) & jnp.logical_not(second))
        def _():
            wait_for(cb.at[p, pl.ds(512, 512)], sem("fc", 0))

        @pl.when((z != p) & even)
        def _():
            wait_for(cb.at[p, pl.ds(0, 512)], sem("pc", 2 * p))

    @pl.when((r == 0) & (z == 1))
    def _():
        wait_for(fb.at[1], sem("fb", 1))

    for b in range(2):
        @pl.when(r == 1)
        def _():
            wait_for(rb.at[b, :, pl.ds(0, 240)], sem("r1s", b))
            wait_for(rb.at[b, :, pl.ds(0, 240)], sem("r2s", b))
            if b == 1:
                wait_for(rb.at[b], sem("rfs", b))

        @pl.when((core == 1) & (chip != 0))
        def _():
            wait_for(rb.at[b, :, pl.ds(0, 224)], sem("r2s", b))
            wait_for(rb.at[b], sem("rfs", b))

    for k in range(4):
        @pl.when(odd & (z == 0))
        def _():
            wait_for(g.at[k, pl.ds(0, 120), width(k)], sem("bs", k))

        @pl.when(odd & (z == 0) & (chip != 0))
        def _():
            wait_for(g.at[k, pl.ds(0, 112), width(k)], sem("cs", k))

        @pl.when(odd & ((z != 0) | (chip == 0)))
        def _():
            wait_for(g.at[k, pl.ds(0, 120), width(k)], sem("cs", k))

        @pl.when(first | (odd & jnp.logical_not(second)))
        def _():
            wait_for(g.at[k, :, width(k)], sem("ss", k))

    for p in range(2):
        own = even & jnp.logical_not(first) if p == 0 else even
        for offset in kids[p]:
            if offset is not None:
                @pl.when((offset != 0) & own)
                def _():
                    wait_for(cb.at[p], sem("zs", p))


def shards(hessian, masses, shift):
    f32 = jnp.float32
    vmem = pl.BlockSpec(memory_space=pltpu.VMEM)
    return pl.pallas_call(
        kernel,
        out_shape=jax.ShapeDtypeStruct(hessian.shape, f32),
        in_specs=[pl.BlockSpec(memory_space=pltpu.SMEM), vmem, vmem],
        out_specs=vmem,
        scratch_shapes=[
            pltpu.VMEM((2, 4, NB, NB), f32),
            pltpu.VMEM((2, 4, NB, NB), f32),
            pltpu.VMEM((2, 4, NB, NB), f32),
            pltpu.VMEM((2, 1024, NB), f32),
            pltpu.VMEM((2, NB, NB), f32),
            pltpu.VMEM((NB, NB), f32),
            pltpu.VMEM((512, 1024), f32),
            pltpu.VMEM((4, 128, 512), f32),
            pltpu.VMEM((512, 512), f32),
            pltpu.VMEM((512, 1024), f32),
            pltpu.VMEM((512, 512), f32),
            pltpu.VMEM((512, 1024), f32),
            pltpu.VMEM((NB, NB), f32),
            pltpu.VMEM((NB, NB), f32),
            pltpu.VMEM((NB, NB), f32),
            pltpu.SemaphoreType.DMA((SEMAPHORES,)),
            pltpu.SemaphoreType.REGULAR((2, 3)),
            pltpu.SemaphoreType.REGULAR((2,)),
            pltpu.SemaphoreType.REGULAR,
        ],
        compiler_params=pltpu.CompilerParams(collective_id=0, has_side_effects=True, vmem_limit_bytes=48 * 2**20),
    )(shift, hessian, masses.reshape(128, 128))


def solution(mesh):
    placed = (P(None, "row", None, "col"), P(), P())
    return jax.shard_map(
        shards, mesh=mesh, in_specs=placed, out_specs=P(None, "row", None, "col"), check_vma=False
    )
```

```python
import functools

import jax
import jax.numpy as jnp
from jax import lax
from jax.experimental import pallas as pl
from jax.experimental.pallas import tpu as pltpu
from jax.sharding import PartitionSpec as P

MESH = pl.DeviceIdType.MESH
HIGHEST = lax.Precision.HIGHEST
Z, R = 16, 32
NB = 256
CHUNKS = 32
ROWS = 1024 // CHUNKS


def wait_for(ref, sem):
    pltpu.make_async_copy(ref, ref, sem).wait()


def lane(x, i):
    return jnp.broadcast_to(x[:, i : i + 1], (8, 128))


def sublane(x, i):
    return jnp.broadcast_to(x[i : i + 1, :], (8, x.shape[1]))


def tree_sum(terms):
    while len(terms) > 1:
        terms = [terms[i] + terms[i + 1] for i in range(0, len(terms), 2)]
    return terms[0]


def factor8(tile, off):
    s, low, inv = {}, {}, {}
    for k in range(8):
        column = lane(tile, off + k)
        for i in range(k, 8):
            s[i, k] = sublane(column, i)
    for j in range(8):
        root = lax.rsqrt(s[j, j])
        for i in range(j + 1, 8):
            low[i, j] = s[i, j] * root
        for k in range(j + 1, 8):
            for i in range(k, 8):
                s[i, k] = s[i, k] - low[i, j] * low[k, j]
        inv[j, j] = root
        for c in range(j):
            total = low[j, c] * inv[c, c]
            for k in range(c + 1, j):
                total = total + low[j, k] * inv[k, c]
            inv[j, c] = -(total * root)
    row = lax.broadcasted_iota(jnp.int32, (8, 128), 0)
    columns = []
    for c in range(8):
        x = jnp.zeros((8, 128), jnp.float32)
        for i in range(c, 8):
            x = jnp.where(row == i, inv[i, c], x)
        columns.append(x)
    return columns


def combine(columns, x):
    return tree_sum([columns[j] * sublane(x, j) for j in range(8)])


def factor128(block, inverse_ref):
    rows = lax.broadcasted_iota(jnp.int32, (8, 128), 0)
    lanes = lax.broadcasted_iota(jnp.int32, (8, 128), 1)
    d = [block[8 * t : 8 * t + 8, :] for t in range(16)]
    e = [jnp.where(lanes == rows + 8 * t, 1.0, 0.0) for t in range(16)]
    for t in range(16):
        columns = factor8(d[t], 8 * t)
        u = combine(columns, d[t])
        f = combine(columns, e[t])
        inverse_ref[8 * t : 8 * t + 8, :] = f
        if t == 15:
            break
        v = u.T
        ub = [sublane(u, j) for j in range(8)]
        fb = [sublane(f, j) for j in range(8)]
        for q in range(t + 1, 16):
            vq = v[8 * q : 8 * q + 8, :]
            g = [lane(vq, j) for j in range(8)]
            d[q] = d[q] - tree_sum([g[j] * ub[j] for j in range(8)])
            e[q] = e[q] - tree_sum([g[j] * fb[j] for j in range(8)])


def split(x):
    high = x.astype(jnp.bfloat16)
    return high, (x - high.astype(jnp.float32)).astype(jnp.bfloat16)


def dot(a, b):
    return jnp.dot(a, b, preferred_element_type=jnp.float32)


NAMES = {}
_TOTAL = 0
for _name, _count in (("in", 2), ("x", 2), ("fc", 2), ("fb", 4), ("pc", 4), ("r1s", 2), ("r1r", 2), ("r2s", 2), ("r2r", 2), ("rfs", 2), ("rfr", 2),
                      ("as", 4), ("ar", 4), ("bs", 4), ("br", 4), ("cs", 4), ("cr", 4), ("ss", 4), ("sr", 4),
                      ("zs", 2), ("ps", 1), ("zr", 2 * CHUNKS)):
    NAMES[_name] = _TOTAL
    _TOTAL += _count
SEMAPHORES = _TOTAL


def rows16(i):
    return pl.ds(pl.multiple_of(16 * i, 16), 16)


def dot3(a, b):
    ah, al = split(a)
    bh, bl = split(b)
    return dot(ah, bh) + dot(ah, bl) + dot(al, bh)


def kernel(shift, h_in, masses_in, out, h, masses, x, acc, rb, cb, fb, tb, w, g, wc, wr, bel, acr, mi, u, ut, sems, ready_z, ready_p, ready_b):
    r, z = lax.axis_index("row"), lax.axis_index("col")
    chip, core = lax.div(r, 2), lax.rem(r, 2)
    even = core == 0
    first = (r == 0) & (z == 0)
    second = (r == 1) & (z == 0)
    odd = core == 1
    sibling = (r + 1 - 2 * core, z)
    zp = [z, lax.rem(z + Z - 1, Z)]

    def sem(name, i=0):
        return sems.at[NAMES[name] + i]

    def col(offset, row=None):
        return (r if row is None else row, lax.rem(z + offset + Z, Z))

    def chip_at(i):
        return (2 * i + core, z)

    def send(src, dst, send_sem, recv_sem, device):
        pltpu.make_async_remote_copy(src, dst, send_sem, recv_sem, device_id=device, device_id_type=MESH).start()

    def signal(s, device):
        pl.semaphore_signal(s, inc=1, device_id=device, device_id_type=MESH)

    def each(low, high, fn):
        def body(i, carry):
            fn(i)
            return carry
        lax.fori_loop(low, high, body, 0)

    def pick(value, cases, default=0):
        result = default
        for key, v in cases.items():
            result = jnp.where(value == key, v, result)
        return result

    def children(p):
        v = zp[p]
        near = {1: 2} if p == 1 else {15: -2}
        fwd = pick(v, {0: 1, 3: 2, 5: 2, 7: 1, 13: -2, 11: -2, 9: 1, **near})
        back = pick(v, {0: -1, 3: -1, 5: -1, 7: -1, 13: 1, 11: 1})
        far = pick(v, {0: -3 if p == 1 else 3})
        return fwd, back, far

    def parent(p):
        v = zp[p]
        offset = pick(v, {1: -1, 15: 1, 3: -2 if p == 1 else -3, 5: -2, 7: -2, 8: -1, 2: 1, 4: 1, 6: 1,
                          13: 3 if p == 1 else 2, 11: 2, 9: 2, 14: -1, 12: -1, 10: -1})
        slot = pick(v, {15: 1, 2: 1, 4: 1, 6: 1, 14: 1, 12: 1, (13 if p == 1 else 3): 2})
        return offset, slot

    kids = [children(0), children(1)]
    from_proxy = (r == 0) & ((z == 1) | (z == 3) | (z == 15))

    load = pltpu.make_async_copy(h_in, h, sem("in", 0))
    load.start()
    load_masses = pltpu.make_async_copy(masses_in, masses, sem("in", 1))
    load_masses.start()

    barrier = pltpu.get_barrier_semaphore()
    signal(barrier, sibling)

    @pl.when(odd)
    def _():
        each(1, 16, lambda i: signal(barrier, chip_at(lax.rem(chip + i, 16))))

    for p in range(2):
        own = even & jnp.logical_not(first) if p == 0 else even
        for offset in kids[p]:
            if offset is not None:
                @pl.when((offset != 0) & own)
                def _():
                    signal(barrier, col(offset))

    @pl.when(second)
    def _():
        signal(barrier, (0, 1))
        signal(barrier, (0, 15))
        signal(barrier, (0, 3))

    @pl.when(odd & (z == 0))
    def _():
        each(1, Z, lambda i: signal(barrier, col(i)))

    one = jnp.int32(1)
    zero = jnp.int32(0)
    expected = (one + jnp.where(odd, 15, 0)
                + jnp.where(even & (zp[0] != 0), one, zero) + jnp.where(even & (zp[1] != 0), one, zero) + jnp.where(odd & (z != 0), one, zero))

    pl.semaphore_wait(barrier, expected)

    for p in range(2):
        offset, slot = parent(p)
        for s in range(3):
            if p == 0:
                @pl.when(even & (zp[p] != 0) & (slot == s) & jnp.logical_not(from_proxy))
                def _():
                    signal(ready_z.at[p, s], col(offset))
            else:
                @pl.when(even & (zp[p] != 0) & (slot == s))
                def _():
                    signal(ready_z.at[p, s], col(offset))

    @pl.when((r == 0) & (z == 1))
    def _():
        signal(ready_p.at[0], (1, 0))

    @pl.when((r == 0) & (z == 15))
    def _():
        signal(ready_p.at[1], (1, 0))

    @pl.when((r == 0) & (z == 3))
    def _():
        signal(ready_p.at[2], (1, 0))

    @pl.when(odd & (z != 0))
    def _():
        signal(ready_b, (r, 0))

    load_masses.wait()
    load.wait()

    def weights(block):
        return 1.0 / jnp.sqrt(masses[pl.ds(2 * block, 2), :])

    across_weights = [weights(z + Z * c) for c in range(4)]
    square = lax.broadcasted_iota(jnp.int32, (NB, NB), 0) == lax.broadcasted_iota(jnp.int32, (NB, NB), 1)
    for k in range(2):
        down = weights(r + R * k)
        for half in range(2):
            tall = jnp.broadcast_to(down[half : half + 1, :], (128, 128)).T
            rows = slice(128 * half, 128 * half + 128)
            for c in range(4):
                for side in range(2):
                    cols = slice(128 * side, 128 * side + 128)
                    x[k, c, rows, cols] = h[k, rows, c, cols] * tall * across_weights[c][side : side + 1, :]
        for c in range(4):
            @pl.when(r + R * k == z + Z * c)
            def _():
                x[k, c] = x[k, c] + jnp.where(square, shift[0], 0.0)

    def chunk_of(i):
        return pl.ds(pl.multiple_of(i * ROWS, ROWS), ROWS)

    def chain_send(p, i, offset):
        piece = cb.at[p, chunk_of(i)]
        send(piece, piece, sem("zs", p), sem("zr", p * CHUNKS + i), col(offset))

    def all_chunks(p, slot, offset):
        pl.semaphore_wait(ready_z.at[p, slot], 1)
        each(0, CHUNKS, lambda i: chain_send(p, i, offset))

    def pumps(p):
        fwd, back, _ = kids[p]

        @pl.when(fwd != 0)
        def _():
            pl.semaphore_wait(ready_z.at[p, 0], 1)

        @pl.when(back != 0)
        def _():
            pl.semaphore_wait(ready_z.at[p, 1], 1)

        def pump(i):
            wait_for(cb.at[p, chunk_of(i)], sem("zr", p * CHUNKS + i))

            @pl.when(fwd != 0)
            def _():
                chain_send(p, i, fwd)

            @pl.when(back != 0)
            def _():
                chain_send(p, i, back)

        each(0, CHUNKS, pump)
        theirs = cb.at[p, pl.ds(512, 512)]
        send(theirs, cb.at[p, pl.ds(0, 512)], sem("pc", 2 * p), sem("pc", 2 * p + 1), sibling)

    def width(k):
        return pl.ds(0, 512 - 128 * k)

    def slab(k, i):
        return g.at[k, pl.ds(pl.multiple_of(8 * i, 8), 8), width(k)]

    def g_relay(k):
        piece = slab(k, chip)

        @pl.when(second)
        def _():
            wait_for(g.at[k, :, width(k)], sem("sr", k))
            each(1, 16, lambda i: send(slab(k, i), slab(k, i), sem("as", k), sem("ar", k), chip_at(i)))

        @pl.when((z == 0) & (chip != 0))
        def _():
            wait_for(piece, sem("ar", k))

        @pl.when(z == 0)
        def _():
            if k == 0:
                pl.semaphore_wait(ready_b, Z - 1)
            each(1, Z, lambda i: send(piece, piece, sem("bs", k), sem("br", k), (r, 1 + lax.rem(i + 6, Z - 1))))

        @pl.when(z != 0)
        def _():
            wait_for(piece, sem("br", k))

        def spread(i):
            there = lax.rem(chip + i, 16)

            @pl.when((z != 0) | (there != 0))
            def _():
                send(piece, piece, sem("cs", k), sem("cr", k), chip_at(there))

        each(1, 16, spread)

    def g_arrive(k):
        whole = g.at[k, :, width(k)]

        @pl.when(jnp.logical_not(second))
        def _():
            wait_for(g.at[k, pl.ds(0, 120), width(k)], sem("cr", k))
            send(whole, whole, sem("ss", k), sem("sr", k), sibling)

    nt = (((1,), (1,)), ((), ()))

    def load_rows(b):
        @pl.when(even & (chip != 0) if b == 0 else even)
        def _():
            wait_for(rb.at[b], sem("rfr", b))

        for c in range(4):
            wr[NB * b : NB * b + NB, NB * c : NB * c + NB] = rb[b, c]

    def invert(q):
        top, bottom = g[2 * q, :, 0:128], g[2 * q + 1, :, 0:128]
        mi[0:128, 0:128] = top
        mi[0:128, 128:256] = jnp.zeros((128, 128), jnp.float32)
        mi[128:256, 128:256] = bottom
        inner = jnp.dot(g[2 * q, :, 128:256].T, top, precision=HIGHEST)
        mi[128:256, 0:128] = -jnp.dot(bottom, inner, precision=HIGHEST)

    def solve_across(q):
        def body(c, carry):
            cols = pl.ds(pl.multiple_of(c * NB, NB), NB)
            acr[NB * q : NB * q + NB, cols] = dot3(mi[...], wr[NB * q : NB * q + NB, cols])
            return carry
        lax.fori_loop(0, 4, body, 0)

    def solve_below(q):
        def body(k, carry):
            rows = pl.ds(pl.multiple_of(k * NB, NB), NB)
            here = slice(NB * q, NB * q + NB)
            bel[rows, here] = lax.dot_general(wc[rows, here], mi[...], nt, precision=HIGHEST)
            return carry
        lax.fori_loop(0, 2, body, 0)

    def update():
        u[0:128, :] = g[0, :, 256:512]
        u[128:256, :] = g[1, :, 128:384]
        ut[...] = u[...].T

        def below_part(k, carry):
            rows = pl.ds(pl.multiple_of(k * NB, NB), NB)
            wc[rows, NB : 2 * NB] = -dot3(bel[rows, 0:NB], u[...])
            return carry
        lax.fori_loop(0, 2, below_part, 0)

        def across_part(c, carry):
            cols = pl.ds(pl.multiple_of(c * NB, NB), NB)
            wr[NB : 2 * NB, cols] = wr[NB : 2 * NB, cols] - dot3(ut[...], acr[0:NB, cols])
            return carry
        lax.fori_loop(0, 4, across_part, 0)

    def product(q):
        def body(k, carry):
            rows = pl.ds(pl.multiple_of(k * NB, NB), NB)
            bh, bl = split(bel[rows, NB * q : NB * q + NB])
            for c in range(4):
                ah, al = split(acr[NB * q : NB * q + NB, NB * c : NB * c + NB])
                term = dot(bh, ah) + dot(bh, al) + dot(bl, ah)
                if q == 0:
                    acc[k, c] = x[k, c] - term
                else:
                    out[k, :, c, :] = acc[k, c] - term
            return carry
        lax.fori_loop(0, 2, body, 0)

    @pl.when(first)
    def _():
        send(x.at[0], rb.at[0], sem("x", 0), sem("x", 1), sibling)
        for k in range(2):
            send(x.at[k, 0], cb.at[0, pl.ds(NB * k, NB)], sem("fc", 0), sem("fc", 1), sibling)
        w[0:NB, 0:NB] = x[0, 0]

        def step(k, carry):
            mine = pl.ds(pl.multiple_of(k * 128, 128), 128)
            window = pl.ds(pl.multiple_of(k * 128 + 128, 128), 384)

            @pl.when(k == 2)
            def _():
                u[0:128, :] = g[0, :, 256:512]
                u[128:256, :] = g[1, :, 128:384]
                wait_for(fb.at[1], sem("fb", 3))
                w[NB : 2 * NB, NB : 2 * NB] = fb[1] - jnp.dot(u[...].T, u[...], precision=HIGHEST)

            factor128(w.at[mine, mine], g.at[k, :, pl.ds(0, 128)])

            @pl.when(k == 0)
            def _():
                wait_for(fb.at[0], sem("fb", 2))
                w[0:NB, NB : 2 * NB] = fb[0]

            @pl.when(k < 3)
            def _():
                g[k, :, 128:512] = jnp.dot(g[k, :, 0:128], w[mine, window], precision=HIGHEST)

            for n in range(4):
                @pl.when(k == n)
                def _():
                    whole = g.at[n, :, width(n)]
                    send(whole, whole, sem("ss", n), sem("sr", n), sibling)

            @pl.when(lax.rem(k, 2) == 0)
            def _():
                there = pl.ds(pl.multiple_of(k * 128 + 128, 128), 128)
                w[there, window] = w[there, window] - jnp.dot(g[k, :, 128:256].T, g[k, :, 128:512], precision=HIGHEST)

            return carry

        lax.fori_loop(0, 4, step, 0)

    @pl.when((r == 0) & (z != 0))
    def _():
        send(x.at[0], rb.at[0], sem("x", 0), sem("x", 1), sibling)

    @pl.when(second)
    def _():
        tb[...] = x[0, 0].T
        send(tb, fb.at[0], sem("fb", 0), sem("fb", 2), sibling)

    for p in range(2):
        @pl.when((z == p) & (core == 1) & jnp.logical_not(second))
        def _():
            for k in range(2):
                send(x.at[k, 0], cb.at[p, pl.ds(512 + NB * k, NB)], sem("fc", 0), sem("fc", 1), sibling)

    @pl.when(r == 0)
    def _():
        rb[0] = x[0]

    @pl.when(r == 1)
    def _():
        rb[1] = x[0]

    def scatter(b):
        def body(i):
            piece = rb.at[b, :, rows16(i)]
            send(piece, piece, sem("r1s", b), sem("r1r", b), chip_at(i))
        each(1, 16, body)

    def gather(b):
        mine = rb.at[b, :, rows16(chip)]

        @pl.when(chip != 0)
        def _():
            wait_for(mine, sem("r1r", b))

        def spread(i):
            there = lax.rem(chip + i, 16)

            @pl.when(there != 0)
            def _():
                send(mine, mine, sem("r2s", b), sem("r2r", b), chip_at(there))

        each(1, 16, spread)

    @pl.when(r == 1)
    def _():
        @pl.when(z == 0)
        def _():
            scatter(1)

        wait_for(rb.at[0], sem("x", 1))
        scatter(0)

        @pl.when(z != 0)
        def _():
            scatter(1)

    def proxy(slot, device):
        pl.semaphore_wait(ready_p.at[slot], 1)

        def body(i):
            piece = cb.at[0, chunk_of(i)]
            send(piece, piece, sem("ps"), sem("zr", i), device)
        each(0, CHUNKS, body)

    @pl.when(second)
    def _():
        for k in range(2):
            cb[0, 512 + NB * k : 512 + NB * k + NB, :] = x[k, 0]
        wait_for(cb.at[0, pl.ds(0, 512)], sem("fc", 1))
        proxy(2, (0, 3))

    @pl.when(odd)
    def _():
        gather(0)
        gather(1)

    @pl.when(second)
    def _():
        proxy(1, (0, 15))
        proxy(0, (0, 1))

    for p in range(2):
        @pl.when((z == p) & even & jnp.logical_not(first))
        def _():
            for k in range(2):
                cb[p, NB * k : NB * k + NB, :] = x[k, 0]
            wait_for(cb.at[p, pl.ds(512, 512)], sem("fc", 1))

    @pl.when((z == 0) & even & jnp.logical_not(first))
    def _():
        all_chunks(0, 2, 3)
        all_chunks(0, 1, -1)
        all_chunks(0, 0, 1)

    @pl.when((z == 1) & even)
    def _():
        all_chunks(1, 0, 1)
        pl.semaphore_wait(ready_z.at[1, 1], 1)

        @pl.when(r == 0)
        def _():
            send(cb.at[1, pl.ds(512, NB)], fb.at[1], sem("fb", 1), sem("fb", 3), (0, 0))

        all_chunks(1, 2, -3)
        each(0, CHUNKS, lambda i: chain_send(1, i, -1))

    leaf = (kids[1][0] == 0) & (kids[1][1] == 0)

    @pl.when((z != 1) & even & jnp.logical_not(leaf))
    def _():
        pumps(1)

    @pl.when((z != 0) & even)
    def _():
        pumps(0)

    def rows_arrive(b):
        @pl.when(core == 1)
        def _():
            @pl.when(chip != 0)
            def _():
                wait_for(rb.at[b, :, pl.ds(0, 240)], sem("r2r", b))

            if b == 0:
                @pl.when(chip != 0)
                def _():
                    send(rb.at[b], rb.at[b], sem("rfs", b), sem("rfr", b), sibling)
            else:
                send(rb.at[b], rb.at[b], sem("rfs", b), sem("rfr", b), sibling)

    @pl.when(odd)
    def _():
        g_relay(0)
        g_relay(1)
        rows_arrive(0)
        g_arrive(0)
        g_relay(2)
        g_arrive(1)

    load_rows(0)

    def load_column(p):
        @pl.when(odd & (z != p))
        def _():
            wait_for(cb.at[p, pl.ds(0, 512)], sem("pc", 2 * p + 1))

        here = slice(NB * p, NB * p + NB)
        for k in range(2):
            rows = slice(NB * k, NB * k + NB)
            old = wc[rows, here] if p else 0.0

            @pl.when(z == p)
            def _():
                wc[rows, here] = x[k, 0] + old

            @pl.when(z != p)
            def _():
                wc[rows, here] = cb[p, rows, :] + old

    load_column(0)

    def slabs_arrive(q):
        @pl.when(even & jnp.logical_not(first))
        def _():
            for k in (2 * q, 2 * q + 1):
                wait_for(g.at[k, :, width(k)], sem("sr", k))

    slabs_arrive(0)
    invert(0)
    solve_across(0)
    solve_below(0)

    @pl.when(odd)
    def _():
        rows_arrive(1)

        @pl.when(z == 0)
        def _():
            g_relay(3)

    load_rows(1)
    update()
    product(0)

    @pl.when(odd)
    def _():
        @pl.when(z != 0)
        def _():
            g_relay(3)

        g_arrive(2)
        g_arrive(3)

    @pl.when((z != 1) & even & leaf)
    def _():
        pumps(1)

    load_column(1)
    slabs_arrive(1)
    invert(1)
    solve_across(1)
    solve_below(1)
    product(1)

    tri = lax.broadcasted_iota(jnp.int32, (NB, NB), 0) >= lax.broadcasted_iota(jnp.int32, (NB, NB), 1)
    for p in range(2):
        @pl.when(z == p)
        def _():
            for k in range(2):
                out[k, :, 0, :] = bel[NB * k : NB * k + NB, NB * p : NB * p + NB]

    for p in range(2):
        @pl.when(r == p)
        def _():
            for c in range(1, 4):
                out[0, :, c, :] = jnp.zeros((NB, NB), jnp.float32)

            @pl.when(z > p)
            def _():
                out[0, :, 0, :] = jnp.zeros((NB, NB), jnp.float32)

            @pl.when(z == p)
            def _():
                out[0, :, 0, :] = jnp.where(tri, bel[0:NB, NB * p : NB * p + NB], 0.0)

    @pl.when(r == 0)
    def _():
        wait_for(x.at[0], sem("x", 0))

    @pl.when(first)
    def _():
        wait_for(cb.at[0, pl.ds(0, 512)], sem("fc", 0))

    @pl.when(second)
    def _():
        for k in range(4):
            wait_for(g.at[k, pl.ds(0, 120), width(k)], sem("as", k))
        wait_for(tb, sem("fb", 0))
        wait_for(rb, sem("ps"))
        wait_for(rb.at[0], sem("ps"))

    for p in range(2):
        @pl.when((z == p) & (core == 1) & jnp.logical_not(second))
        def _():
            wait_for(cb.at[p, pl.ds(512, 512)], sem("fc", 0))

        @pl.when((z != p) & even)
        def _():
            wait_for(cb.at[p, pl.ds(0, 512)], sem("pc", 2 * p))

    @pl.when((r == 0) & (z == 1))
    def _():
        wait_for(fb.at[1], sem("fb", 1))

    for b in range(2):
        @pl.when(r == 1)
        def _():
            wait_for(rb.at[b, :, pl.ds(0, 240)], sem("r1s", b))
            wait_for(rb.at[b, :, pl.ds(0, 240)], sem("r2s", b))
            if b == 1:
                wait_for(rb.at[b], sem("rfs", b))

        @pl.when((core == 1) & (chip != 0))
        def _():
            wait_for(rb.at[b, :, pl.ds(0, 224)], sem("r2s", b))
            wait_for(rb.at[b], sem("rfs", b))

    for k in range(4):
        @pl.when(odd & (z == 0))
        def _():
            wait_for(g.at[k, pl.ds(0, 120), width(k)], sem("bs", k))

        @pl.when(odd & (z == 0) & (chip != 0))
        def _():
            wait_for(g.at[k, pl.ds(0, 112), width(k)], sem("cs", k))

        @pl.when(odd & ((z != 0) | (chip == 0)))
        def _():
            wait_for(g.at[k, pl.ds(0, 120), width(k)], sem("cs", k))

        @pl.when(first | (odd & jnp.logical_not(second)))
        def _():
            wait_for(g.at[k, :, width(k)], sem("ss", k))

    for p in range(2):
        own = even & jnp.logical_not(first) if p == 0 else even
        for offset in kids[p]:
            if offset is not None:
                @pl.when((offset != 0) & own)
                def _():
                    wait_for(cb.at[p], sem("zs", p))


def shards(hessian, masses, shift):
    f32 = jnp.float32
    vmem = pl.BlockSpec(memory_space=pltpu.VMEM)
    anywhere = pl.BlockSpec(memory_space=pltpu.HBM)
    return pl.pallas_call(
        kernel,
        out_shape=jax.ShapeDtypeStruct(hessian.shape, f32),
        in_specs=[pl.BlockSpec(memory_space=pltpu.SMEM), anywhere, anywhere],
        out_specs=vmem,
        scratch_shapes=[
            pltpu.VMEM(hessian.shape, f32),
            pltpu.VMEM((128, 128), f32),
            pltpu.VMEM((2, 4, NB, NB), f32),
            pltpu.VMEM((2, 4, NB, NB), f32),
            pltpu.VMEM((2, 4, NB, NB), f32),
            pltpu.VMEM((2, 1024, NB), f32),
            pltpu.VMEM((2, NB, NB), f32),
            pltpu.VMEM((NB, NB), f32),
            pltpu.VMEM((512, 1024), f32),
            pltpu.VMEM((4, 128, 512), f32),
            pltpu.VMEM((512, 512), f32),
            pltpu.VMEM((512, 1024), f32),
            pltpu.VMEM((512, 512), f32),
            pltpu.VMEM((512, 1024), f32),
            pltpu.VMEM((NB, NB), f32),
            pltpu.VMEM((NB, NB), f32),
            pltpu.VMEM((NB, NB), f32),
            pltpu.SemaphoreType.DMA((SEMAPHORES,)),
            pltpu.SemaphoreType.REGULAR((2, 3)),
            pltpu.SemaphoreType.REGULAR((3,)),
            pltpu.SemaphoreType.REGULAR,
        ],
        compiler_params=pltpu.CompilerParams(collective_id=0, has_side_effects=True, vmem_limit_bytes=32 * 2**20),
    )(shift, hessian, masses.reshape(128, 128))


def solution(mesh):
    placed = (P(None, "row", None, "col"), P(), P())
    return jax.shard_map(
        shards, mesh=mesh, in_specs=placed, out_specs=P(None, "row", None, "col"), check_vma=False
    )
```
